512 devices in a mesh: frame: 128 (over x, z, core), head: 4 (over y).
Axes of the slice: x: 4, y: 4, z: 16, core: 2. Of those that a mesh axis runs over, the one named last changes fastest.
Arguments:
- queries: bfloat16 [256, 384, 1024], P('frame', None, 'head'), may hold values from -12 to 12
- keys: bfloat16 [256, 384, 1024], P('frame', None, 'head'), may hold values from -5 to 5
- values: bfloat16 [256, 384, 1024], P('frame', None, 'head'), may hold values from -6 to 6
- pairs: int32 [256, 2], replicated, may hold values from 0 to 255, as said below
- out_weight: bfloat16 [1024, 1024], P('head'), may hold values from -0.1875 to 0.1875
Outputs:
- mixed: bfloat16 [256, 384, 1024], P('frame', None, 'head')
The draws below stay inside these ranges and needn't reach their ends.
Inputs may be any that keep to these rules, and one draw needn't show every extreme that they name: `pairs`: each row (a, b) names two frames with a < b <= a + 2; no two rows name the same pair.
All inputs are finite; a program needn't handle non-finite values.
Results may differ from the reference program's by a relative error of at most 0.019.
Values may be sent and summed in bfloat16 or wider, within the bound.
A program may use at most 64 MiB of HBM per device.

```python
import jax
import jax.numpy as jnp
from jax import lax

H = 16
HD = 64
D = 1024
P_SIZE = 384
SPAN = 2
FRAMES = 256
NPAIR = 256
N_HEAD = 4


def draw_queries(key, part):
    key = jax.random.fold_in(key, 11)
    result = jnp.clip(jax.random.normal(key, (FRAMES, P_SIZE, D), jnp.float32), -5.0, 5.0)
    return result.astype(jnp.bfloat16)


def draw_keys(key, part):
    key = jax.random.fold_in(key, 12)
    result = jnp.clip(jax.random.normal(key, (FRAMES, P_SIZE, D), jnp.float32), -5.0, 5.0)
    return result.astype(jnp.bfloat16)


def draw_pairs(key, part):
    key = jax.random.fold_in(key, 13)
    hub_flags = (jax.random.randint(jax.random.fold_in(key, 1), (FRAMES,), 0, 4) == 0).astype(jnp.int32)
    candidate = jnp.arange(FRAMES * SPAN, dtype=jnp.int32)
    lower_end = candidate // SPAN
    upper_end = lower_end + candidate % SPAN + 1
    usable = upper_end < FRAMES
    upper_safe = jnp.minimum(upper_end, FRAMES - 1)
    jitter = jax.random.randint(jax.random.fold_in(key, 2), (FRAMES * SPAN,), 0, 1024)
    hub_count = hub_flags[lower_end] + hub_flags[upper_safe]
    priority = jnp.where(usable, 1 + jitter + 1024 * hub_count, 0)
    distinct = priority * (FRAMES * SPAN) + candidate
    chosen = lax.top_k(distinct, NPAIR)[1]
    return jnp.stack([lower_end[chosen], upper_end[chosen]], 1).astype(jnp.int32)


def block_levels(key, dims, pieces, low, largest):
    loudness, own = 1.0, jax.random.fold_in(key, 6)
    for axis_at, parts in pieces:
        draws = jnp.exp(jax.random.uniform(jax.random.fold_in(own, axis_at), (parts,), jnp.float32, low / len(pieces), largest / len(pieces)))
        loudness = loudness * jnp.repeat(draws, dims[axis_at] // parts).reshape([-1 if axis == axis_at else 1 for axis in range(len(dims))])
    return loudness


def bell_draw(key, shape, scale, reach, cuts=(), kind=jnp.bfloat16):
    factor_of = block_levels(key, shape, cuts, -0.22, 0.18) if cuts else 1.0
    array = jax.random.normal(key, shape, jnp.float32) * scale * factor_of
    return jnp.minimum(jnp.maximum(array, -reach), reach).astype(kind)


def setup_inputs(seed: int = 0) -> dict:
    arg_keys = jax.random.split(jax.random.key(seed), 6)
    queries = draw_queries(jax.random.fold_in(arg_keys[5], 71), 0)
    keys = draw_keys(jax.random.fold_in(arg_keys[5], 71), 0)
    values = bell_draw(arg_keys[2], (FRAMES, P_SIZE, D), 1.0, 6.0, ((0, 128), (2, 4)))
    pairs = draw_pairs(jax.random.fold_in(arg_keys[5], 71), 0)
    out_weight = bell_draw(arg_keys[4], (D, D), D ** -0.5, 0.1875, ((0, 4),))
    return dict(queries=queries, keys=keys, values=values, pairs=pairs, out_weight=out_weight)


def attend(query, key_frame, value_frame):
    scores = jnp.einsum("phd,khd->hpk", query.astype(jnp.float32), key_frame.astype(jnp.float32)) * 0.125
    row_top = jnp.max(scores, axis=-1)
    weights = lax.optimization_barrier(jnp.exp(scores - row_top[..., None]).astype(jnp.bfloat16))
    row_total = jnp.sum(weights.astype(jnp.float32), axis=-1)
    summed = jnp.einsum("hpk,khd->phd", weights.astype(jnp.float32), value_frame.astype(jnp.float32))
    partial_value = lax.optimization_barrier((summed / row_total.T[:, :, None]).astype(jnp.bfloat16))
    log_mass = (row_top + jnp.log(row_total)).T
    return partial_value, log_mass


def combine_states(states, partial_value, log_mass):
    peak_lse, weight_sum, weighted = states
    newest = jnp.maximum(peak_lse, log_mass)
    old_scale = jnp.exp(peak_lse - newest)
    new_scale = jnp.exp(log_mass - newest)
    return (newest, weight_sum * old_scale + new_scale,
            weighted * old_scale[..., None] + new_scale[..., None] * partial_value.astype(jnp.float32))


def reference(queries, keys, values, pairs, out_weight):
    query_frames = queries.reshape(FRAMES, P_SIZE, H, HD)
    key_frames = keys.reshape(FRAMES, P_SIZE, H, HD)
    value_frames = values.reshape(FRAMES, P_SIZE, H, HD)

    def self_block(triple):
        partial_value, log_mass = attend(triple[0], triple[1], triple[2])
        return log_mass, jnp.ones_like(log_mass), partial_value.astype(jnp.float32)

    states = lax.map(self_block, (query_frames, key_frames, value_frames))

    def add_block(states, query_index, key_index):
        partial_value, log_mass = attend(query_frames[query_index], key_frames[key_index], value_frames[key_index])
        current = tuple(member[query_index] for member in states)
        merged = combine_states(current, partial_value, log_mass)
        return tuple(member.at[query_index].set(update) for member, update in zip(states, merged))

    def visit_pair(states, pair_row):
        states = add_block(states, pair_row[0], pair_row[1])
        states = add_block(states, pair_row[1], pair_row[0])
        return states, jnp.zeros((), jnp.int32)

    states = lax.scan(visit_pair, states, pairs)[0]
    attention = (states[2] / states[1][..., None]).astype(jnp.bfloat16).reshape(FRAMES * P_SIZE, D)
    group_cols = D // N_HEAD

    def add_group(group, running):
        start = group * group_cols
        columns = lax.dynamic_slice_in_dim(attention, start, group_cols, 1)
        weight_rows = lax.dynamic_slice_in_dim(out_weight, start, group_cols, 0)
        piece = jnp.dot(columns, weight_rows, preferred_element_type=jnp.float32).astype(jnp.bfloat16)
        piece = lax.optimization_barrier(piece)
        return running + piece.astype(jnp.float32)

    summed = lax.fori_loop(0, N_HEAD, add_group, jnp.zeros((FRAMES * P_SIZE, D), jnp.float32))
    return summed.astype(jnp.bfloat16).reshape(FRAMES, P_SIZE, D)
```

```python
import functools

import jax
import jax.numpy as jnp
from jax import lax
from jax.experimental import pallas as pl
from jax.experimental.pallas import tpu as pltpu
from jax.sharding import PartitionSpec as P

HD = 64
PAIR = 2 * HD
LOG2E = 1.4426950408889634
FAR = 1.0e5
MESH = pl.DeviceIdType.MESH
F32 = jnp.float32
BF16 = jnp.bfloat16
ACROSS = (((1,), (1,)), ((), ()))

PARTNER_FAR, PARTNER_NEAR, INNER, OUTER, NEXT_NEAR, NEXT_FAR = range(6)


def kernel(
    frames_axis,
    groups,
    q_hbm,
    k_hbm,
    v_hbm,
    pairs_ref,
    w_hbm,
    out_hbm,
    q_raw,
    q_cut,
    k_all,
    v_all,
    penalty,
    acc,
    top,
    gathered,
    w_all,
    mixed,
    send_sem,
    recv_sem,
    local_sem,
):
    tokens = q_hbm.shape[1]
    group_cols = q_hbm.shape[2]
    me = lax.axis_index("frame")
    group = lax.axis_index("head")
    core = lax.rem(me, 2)
    toward = 1 - 2 * core
    partner = me + toward
    beyond = lax.rem(me - toward + frames_axis, frames_axis)
    up = lax.rem(group + 1, groups)
    down = lax.rem(group + groups - 1, groups)
    across = lax.rem(group + 2, groups)
    outer = core
    inner = 1 - core

    barrier = pltpu.get_barrier_semaphore()
    for device in (
        (partner, group),
        (beyond, group),
        (me, up),
        (me, down),
        (me, across),
    ):
        pl.semaphore_signal(barrier, inc=1, device_id=device, device_id_type=MESH)

    def fetch(number, source, target):
        copy = pltpu.make_async_copy(source, target, local_sem.at[number])
        copy.start()
        return copy

    own_q = fetch(0, q_hbm, q_raw)
    own_kv = []
    for slot, frame in ((INNER, inner), (OUTER, outer)):
        for p in range(2):
            for which, (source, target) in enumerate(((k_hbm, k_all), (v_hbm, v_all))):
                own_kv.append(
                    fetch(
                        1 + len(own_kv),
                        source.at[frame, :, pl.ds(p * PAIR, PAIR)],
                        target.at[slot, p],
                    )
                )
    own_w = fetch(
        9, w_hbm.at[:, pl.ds(pl.multiple_of(group * group_cols, group_cols), group_cols)], w_all.at[0]
    )

    pl.semaphore_wait(barrier, 5)

    sends = []

    def send(source, target, device):
        number = len(sends)
        copy = pltpu.make_async_remote_copy(
            src_ref=source,
            dst_ref=target,
            send_sem=send_sem.at[number],
            recv_sem=recv_sem.at[number],
            device_id=device,
            device_id_type=MESH,
        )
        copy.start()
        sends.append(copy)
        return copy

    next_kv = {}
    for p in range(2):
        for slot, frame in ((NEXT_NEAR, outer), (NEXT_FAR, inner)):
            next_kv[slot, p] = [
                send(
                    source.at[frame, :, pl.ds(p * PAIR, PAIR)],
                    target.at[slot, p],
                    (beyond, group),
                )
                for source, target in ((k_hbm, k_all), (v_hbm, v_all))
            ]
    partner_kv = []
    for slot, frame in ((PARTNER_NEAR, inner), (PARTNER_FAR, outer)):
        for p in range(2):
            partner_kv += [
                send(
                    source.at[frame, :, pl.ds(p * PAIR, PAIR)],
                    target.at[slot, p],
                    (partner, group),
                )
                for source, target in ((k_hbm, k_all), (v_hbm, v_all))
            ]
    w_parts = [
        send(
            w_hbm.at[:, pl.ds(pl.multiple_of(there * group_cols, group_cols), group_cols)],
            w_all.at[place],
            (me, there),
        )
        for place, there in ((1, up), (2, down), (3, across))
    ]

    lower_end = pairs_ref[0:1, :]
    upper_end = pairs_ref[1:2, :]
    own_first = 2 * me

    def place_of(slot):
        steps = (3, 2, 1, 0, -1, -2)[slot]
        return own_first + outer + toward * steps

    for t, slot_q in enumerate((INNER, OUTER)):
        for slot in range(6):
            if slot == slot_q or abs(slot - slot_q) > 2:
                continue
            a, b = place_of(slot_q), place_of(slot)
            hit = (lower_end == jnp.minimum(a, b)) & (upper_end == jnp.maximum(a, b))
            missing = jnp.min(jnp.where(hit, 0.0, FAR).astype(F32), axis=1, keepdims=True)
            penalty[t, slot] = jnp.broadcast_to(missing, (8, PAIR))
        penalty[t, slot_q] = jnp.zeros((8, PAIR), F32)

    lane = lax.broadcasted_iota(jnp.int32, (tokens, PAIR), 1)
    first = lane < HD

    own_q.wait()
    for t, frame in enumerate((inner, outer)):
        for p in range(2):
            q = q_raw[frame, :, p * PAIR : (p + 1) * PAIR].astype(F32) * (0.125 * LOG2E)
            high = q.astype(BF16)
            low = (q - high.astype(F32)).astype(BF16)
            nothing = jnp.zeros_like(high)
            for h in range(2):
                mine = first if h == 0 else ~first
                q_cut[t, p, h, :, 0:PAIR] = jnp.where(mine, high, nothing)
                q_cut[t, p, h, :, PAIR : 2 * PAIR] = jnp.where(mine, low, nothing)

    def attend(t, p, h, low_slot, high_slot, old):
        count = high_slot - low_slot
        k = k_all[low_slot:high_slot, p].reshape(count * tokens, PAIR)
        v = v_all[low_slot:high_slot, p].reshape(count * tokens, PAIR)
        scores = lax.dot_general(
            q_cut[t, p, h], jnp.concatenate([k, k], 1), ACROSS, preferred_element_type=F32
        )
        highest = None
        for j in range(count):
            s = scores[:, j * tokens : (j + 1) * tokens]
            part = s[:, 0:PAIR]
            for c in range(1, tokens // PAIR):
                part = jnp.maximum(part, s[:, c * PAIR : (c + 1) * PAIR])
            part = part - penalty[t, low_slot + j, 0:1, :]
            highest = part if highest is None else jnp.maximum(highest, part)
        now = jnp.broadcast_to(jnp.max(highest, axis=1, keepdims=True), (tokens, PAIR))
        if old is not None:
            now = jnp.maximum(now, old[0])
        weights = []
        for j in range(count):
            less = now + penalty[t, low_slot + j, 0:1, :]
            for c in range(tokens // PAIR):
                at = j * tokens + c * PAIR
                weights.append(jnp.exp2((scores[:, at : at + PAIR] - less).astype(BF16)))
        summed = jnp.dot(
            jnp.concatenate(weights, 1),
            jnp.concatenate([v, jnp.ones_like(v)], 1),
            preferred_element_type=F32,
        )
        if old is not None:
            scale = jnp.exp2(old[0] - now)
            summed = summed + old[1] * jnp.concatenate([scale, scale], 1)
        return now, summed

    for copy in own_kv:
        copy.wait()
    for copy in partner_kv:
        copy.wait_recv()

    def near_frames(p, carry):
        for t, low_slot, high_slot in ((0, 0, 4), (1, 1, 4)):
            for h in range(2):
                now, summed = attend(t, p, h, low_slot, high_slot, None)
                top[t, p, h] = now
                acc[t, p, h] = summed
        return carry

    lax.fori_loop(0, 2, near_frames, 0)

    def finish(t, p, results):
        parts = [summed[:, 0:PAIR] / summed[:, PAIR : 2 * PAIR] for _, summed in results]
        gathered[0, t, p] = jnp.where(first, parts[0], parts[1]).astype(BF16)
        return [
            send(gathered.at[0, t, p], gathered.at[1, t, p], (me, up)),
            send(gathered.at[0, t, p], gathered.at[2, t, p], (me, down)),
        ]

    half = tokens // 2

    def pass_on(t, p, direct):
        for copy in direct:
            copy.wait_recv()
        return [
            send(
                gathered.at[1, t, p, pl.ds(0, half)],
                gathered.at[3, t, p, pl.ds(0, half)],
                (me, up),
            ),
            send(
                gathered.at[2, t, p, pl.ds(half, half)],
                gathered.at[3, t, p, pl.ds(half, half)],
                (me, down),
            ),
        ]

    def project(t, p, source):
        return jnp.dot(
            gathered[source, t, p],
            w_all[source, p * PAIR : (p + 1) * PAIR, :],
            preferred_element_type=F32,
        )

    def project_both(t, source):
        return jnp.dot(
            jnp.concatenate([gathered[source, t, 0], gathered[source, t, 1]], 1),
            w_all[source],
            preferred_element_type=F32,
        )

    def write(t, frame, total):
        mixed[t] = total.astype(BF16)
        return fetch(10 + t, mixed.at[t], out_hbm.at[frame])

    direct, forward = {}, {}
    for p in range(2):
        for copy in next_kv[NEXT_NEAR, p]:
            copy.wait_recv()
        results = [
            attend(0, p, h, NEXT_NEAR, NEXT_NEAR + 1, (top[0, p, h], acc[0, p, h])) for h in range(2)
        ]
        direct[0, p] = finish(0, p, results)
        for h in range(2):
            now, summed = attend(1, p, h, NEXT_NEAR, NEXT_NEAR + 1, (top[1, p, h], acc[1, p, h]))
            top[1, p, h] = now
            acc[1, p, h] = summed
        if p == 1:
            forward[1, 0] = pass_on(1, 0, direct[1, 0])
        for copy in next_kv[NEXT_FAR, p]:
            copy.wait_recv()
        results = [
            attend(1, p, h, NEXT_FAR, NEXT_FAR + 1, (top[1, p, h], acc[1, p, h])) for h in range(2)
        ]
        direct[1, p] = finish(1, p, results)
        forward[0, p] = pass_on(0, p, direct[0, p])

    own_w.wait()
    for copy in w_parts + forward[0, 0] + forward[1, 0]:
        copy.wait_recv()
    total = project(1, 0, 0)
    for source in range(1, 4):
        total = total + project(1, 0, source)
    total = total + project(1, 1, 0)
    forward[1, 1] = pass_on(1, 1, direct[1, 1])
    total = total + project(1, 1, 1) + project(1, 1, 2)
    for copy in forward[0, 1]:
        copy.wait_recv()
    other = project_both(0, 0)
    for source in range(1, 4):
        other = other + project_both(0, source)
    out_inner = write(0, inner, other)
    for copy in forward[1, 1]:
        copy.wait_recv()
    out_outer = write(1, outer, total + project(1, 1, 3))
    for copy in sends:
        copy.wait_send()
    out_inner.wait()
    out_outer.wait()


def body(queries, keys, values, pairs, out_weight):
    own_frames, tokens, cols = queries.shape
    frames_axis = lax.axis_size("frame")
    groups = lax.axis_size("head")
    assert own_frames == 2 and cols == 4 * HD and groups == 4
    anywhere = pl.BlockSpec(memory_space=pl.ANY)
    in_place = pl.BlockSpec(memory_space=pltpu.HBM)
    multiply_adds = 10 * 4 * tokens * tokens * (4 * HD + 4 * HD) + 2 * tokens * groups * cols * cols
    return pl.pallas_call(
        functools.partial(kernel, frames_axis, groups),
        out_shape=jax.ShapeDtypeStruct(queries.shape, BF16),
        in_specs=[in_place] * 3 + [pl.BlockSpec(memory_space=pltpu.VMEM), in_place],
        out_specs=anywhere,
        scratch_shapes=[
            pltpu.VMEM((2, tokens, cols), BF16),
            pltpu.VMEM((2, 2, 2, tokens, 2 * PAIR), BF16),
            pltpu.VMEM((6, 2, tokens, PAIR), BF16),
            pltpu.VMEM((6, 2, tokens, PAIR), BF16),
            pltpu.VMEM((2, 6, 8, PAIR), F32),
            pltpu.VMEM((2, 2, 2, tokens, 2 * PAIR), F32),
            pltpu.VMEM((2, 2, 2, tokens, PAIR), F32),
            pltpu.VMEM((4, 2, 2, tokens, PAIR), BF16),
            pltpu.VMEM((4, cols, cols), BF16),
            pltpu.VMEM((2, tokens, cols), BF16),
            pltpu.SemaphoreType.DMA((35,)),
            pltpu.SemaphoreType.DMA((35,)),
            pltpu.SemaphoreType.DMA((12,)),
        ],
        compiler_params=pltpu.CompilerParams(
            collective_id=0, has_side_effects=True, vmem_limit_bytes=48 * 2**20
        ),
        cost_estimate=pl.CostEstimate(
            flops=2 * multiply_adds, bytes_accessed=4 * queries.size * 2, transcendentals=0
        ),
    )(queries, keys, values, pairs.T, out_weight)


def solution(mesh):
    placed = (
        P("frame", None, "head"),
        P("frame", None, "head"),
        P("frame", None, "head"),
        P(),
        P("head", None),
    )
    return jax.shard_map(
        body, mesh=mesh, in_specs=placed, out_specs=P("frame", None, "head"), check_vma=False
    )
```

```python
import functools

import jax
import jax.numpy as jnp
from jax import lax
from jax.experimental import pallas as pl
from jax.experimental.pallas import tpu as pltpu
from jax.sharding import PartitionSpec as P

HD = 64
PAIR = 2 * HD
LOG2E = 1.4426950408889634
FAR = 1.0e5
RUN = 32
MESH = pl.DeviceIdType.MESH
F32 = jnp.float32
BF16 = jnp.bfloat16
ACROSS = (((1,), (1,)), ((), ()))

PARTNER_FAR, PARTNER_NEAR, INNER, OUTER, NEXT_NEAR, NEXT_FAR = range(6)


def kernel(
    frames_axis,
    groups,
    q_hbm,
    k_hbm,
    v_hbm,
    pairs_ref,
    w_hbm,
    mixed,
    q_raw,
    q_cut,
    k_all,
    v_all,
    penalty,
    acc,
    top,
    gathered,
    w_all,
    send_sem,
    recv_sem,
    local_sem,
    ready,
):
    tokens = q_hbm.shape[1]
    group_cols = q_hbm.shape[2]
    me = lax.axis_index("frame")
    group = lax.axis_index("head")
    core = lax.rem(me, 2)
    toward = 1 - 2 * core
    partner = me + toward
    beyond = lax.rem(me - toward + frames_axis, frames_axis)
    up = lax.rem(group + 1, groups)
    down = lax.rem(group + groups - 1, groups)
    across = lax.rem(group + 2, groups)
    outer = core
    inner = 1 - core
    late = lax.rem(me, RUN) == 0

    barrier = pltpu.get_barrier_semaphore()
    for device in ((partner, group), (me, up), (me, down), (me, across)):
        pl.semaphore_signal(barrier, inc=1, device_id=device, device_id_type=MESH)

    @pl.when(core == 0)
    def _():
        pl.semaphore_signal(barrier, inc=1, device_id=(beyond, group), device_id_type=MESH)

    def fetch(number, source, target):
        copy = pltpu.make_async_copy(source, target, local_sem.at[number])
        copy.start()
        return copy

    own_q = fetch(0, q_hbm, q_raw)
    own_kv = []
    for slot, frame in ((INNER, inner), (OUTER, outer)):
        for p in range(2):
            for which, (source, target) in enumerate(((k_hbm, k_all), (v_hbm, v_all))):
                own_kv.append(
                    fetch(
                        1 + len(own_kv),
                        source.at[frame, :, pl.ds(p * PAIR, PAIR)],
                        target.at[slot, p],
                    )
                )
    own_w = fetch(
        9, w_hbm.at[:, pl.ds(pl.multiple_of(group * group_cols, group_cols), group_cols)], w_all.at[0]
    )

    pl.semaphore_wait(barrier, 4 + core)


    sends = []

    def prepare(source, target, device):
        number = len(sends)
        copy = pltpu.make_async_remote_copy(
            src_ref=source,
            dst_ref=target,
            send_sem=send_sem.at[number],
            recv_sem=recv_sem.at[number],
            device_id=device,
            device_id_type=MESH,
        )
        sends.append(copy)
        return copy

    def send(source, target, device):
        copy = prepare(source, target, device)
        copy.start()
        return copy

    next_kv = {}
    for p in range(2):
        for slot, frame in ((NEXT_NEAR, outer), (NEXT_FAR, inner)):
            next_kv[slot, p] = [
                prepare(
                    source.at[frame, :, pl.ds(p * PAIR, PAIR)],
                    target.at[slot, p],
                    (beyond, group),
                )
                for source, target in ((k_hbm, k_all), (v_hbm, v_all))
            ]

    @pl.when(core == 1)
    def _():
        pl.semaphore_signal(ready, inc=1, device_id=(beyond, group), device_id_type=MESH)
        for copies in next_kv.values():
            for copy in copies:
                copy.start()

    partner_kv = []
    for slot, frame in ((PARTNER_NEAR, inner), (PARTNER_FAR, outer)):
        for p in range(2):
            partner_kv += [
                send(
                    source.at[frame, :, pl.ds(p * PAIR, PAIR)],
                    target.at[slot, p],
                    (partner, group),
                )
                for source, target in ((k_hbm, k_all), (v_hbm, v_all))
            ]
    rows = pl.ds(pl.multiple_of(core * (group_cols // 2), group_cols // 2), group_cols // 2)
    w_parts = [
        send(
            w_hbm.at[rows, pl.ds(pl.multiple_of(there * group_cols, group_cols), group_cols)],
            w_all.at[place, rows],
            (me, there),
        )
        for place, there in ((1, up), (2, down), (3, across))
    ]

    lower_end = pairs_ref[0:1, :]
    upper_end = pairs_ref[1:2, :]
    own_first = 2 * me

    def place_of(slot):
        steps = (3, 2, 1, 0, -1, -2)[slot]
        return own_first + outer + toward * steps

    for t, slot_q in enumerate((INNER, OUTER)):
        for slot in range(6):
            if slot == slot_q or abs(slot - slot_q) > 2:
                continue
            a, b = place_of(slot_q), place_of(slot)
            hit = (lower_end == jnp.minimum(a, b)) & (upper_end == jnp.maximum(a, b))
            missing = jnp.min(jnp.where(hit, 0.0, FAR).astype(F32), axis=1, keepdims=True)
            penalty[t, slot] = jnp.broadcast_to(missing, (8, PAIR))
        penalty[t, slot_q] = jnp.zeros((8, PAIR), F32)

    lane = lax.broadcasted_iota(jnp.int32, (tokens, PAIR), 1)
    first = lane < HD

    own_q.wait()
    for t, frame in enumerate((inner, outer)):
        for p in range(2):
            q = q_raw[frame, :, p * PAIR : (p + 1) * PAIR].astype(F32) * (0.125 * LOG2E)
            high = q.astype(BF16)
            low = (q - high.astype(F32)).astype(BF16)
            nothing = jnp.zeros_like(high)
            for h in range(2):
                mine = first if h == 0 else ~first
                q_cut[t, p, h, :, 0:PAIR] = jnp.where(mine, high, nothing)
                q_cut[t, p, h, :, PAIR : 2 * PAIR] = jnp.where(mine, low, nothing)

    def attend(t, p, h, low_slot, high_slot, old):
        count = high_slot - low_slot
        k = k_all[low_slot:high_slot, p].reshape(count * tokens, PAIR)
        v = v_all[low_slot:high_slot, p].reshape(count * tokens, PAIR)
        scores = lax.dot_general(
            q_cut[t, p, h], jnp.concatenate([k, k], 1), ACROSS, preferred_element_type=F32
        )
        highest = None
        for j in range(count):
            s = scores[:, j * tokens : (j + 1) * tokens]
            part = s[:, 0:PAIR]
            for c in range(1, tokens // PAIR):
                part = jnp.maximum(part, s[:, c * PAIR : (c + 1) * PAIR])
            part = part - penalty[t, low_slot + j, 0:1, :]
            highest = part if highest is None else jnp.maximum(highest, part)
        now = jnp.broadcast_to(jnp.max(highest, axis=1, keepdims=True), (tokens, PAIR))
        if old is not None:
            now = jnp.maximum(now, old[0])
        weights = []
        for j in range(count):
            less = now + penalty[t, low_slot + j, 0:1, :]
            for c in range(tokens // PAIR):
                at = j * tokens + c * PAIR
                weights.append(jnp.exp2((scores[:, at : at + PAIR] - less).astype(BF16)))
        summed = jnp.dot(
            jnp.concatenate(weights, 1),
            jnp.concatenate([v, jnp.ones_like(v)], 1),
            preferred_element_type=F32,
        )
        if old is not None:
            scale = jnp.exp2(old[0] - now)
            summed = summed + old[1] * jnp.concatenate([scale, scale], 1)
        return now, summed

    def start_beyond():
        pl.semaphore_wait(ready, 1)
        for copies in next_kv.values():
            for copy in copies:
                copy.start()

    @pl.when((core == 0) & ~late)
    def _():
        start_beyond()

    for copy in own_kv:
        copy.wait()
    for copy in partner_kv:
        copy.wait_recv()

    def near_frames(p):
        for t, low_slot, high_slot in ((0, 0, 4), (1, 1, 4)):
            for h in range(2):
                now, summed = attend(t, p, h, low_slot, high_slot, None)
                top[t, p, h] = now
                acc[t, p, h] = summed

    def finish(t, p, results):
        parts = [summed[:, 0:PAIR] / summed[:, PAIR : 2 * PAIR] for _, summed in results]
        gathered[0, t, p] = jnp.where(first, parts[0], parts[1]).astype(BF16)
        targets = [(1, up), (2, down)] + ([(3, across)] if (t, p) == (1, 1) else [])
        return [send(gathered.at[0, t, p], gathered.at[place, t, p], (me, there)) for place, there in targets]

    half = tokens // 2

    def pass_on(t, p, direct):
        for copy in direct:
            copy.wait_recv()
        return [
            send(
                gathered.at[1, t, p, pl.ds(0, half)],
                gathered.at[3, t, p, pl.ds(0, half)],
                (me, up),
            ),
            send(
                gathered.at[2, t, p, pl.ds(half, half)],
                gathered.at[3, t, p, pl.ds(half, half)],
                (me, down),
            ),
        ]

    def project(t, *parts):
        return jnp.dot(
            jnp.concatenate([gathered[source, t, p] for source, p in parts], 1),
            jnp.concatenate([w_all[source, p * PAIR : (p + 1) * PAIR, :] for source, p in parts], 0),
            preferred_element_type=F32,
        )

    direct, forward = {}, {}
    for p in range(2):
        if p == 0:
            near_frames(0)

            @pl.when(late)
            def _():
                near_frames(1)
                start_beyond()

        else:

            @pl.when(~late)
            def _():
                near_frames(1)

        for copy in next_kv[NEXT_NEAR, p]:
            copy.wait_recv()
        results = [
            attend(0, p, h, NEXT_NEAR, NEXT_NEAR + 1, (top[0, p, h], acc[0, p, h])) for h in range(2)
        ]
        direct[0, p] = finish(0, p, results)
        for h in range(2):
            now, summed = attend(1, p, h, NEXT_NEAR, NEXT_NEAR + 1, (top[1, p, h], acc[1, p, h]))
            top[1, p, h] = now
            acc[1, p, h] = summed
        if p == 1:
            forward[1, 0] = pass_on(1, 0, direct[1, 0])
        for copy in next_kv[NEXT_FAR, p]:
            copy.wait_recv()
        results = [
            attend(1, p, h, NEXT_FAR, NEXT_FAR + 1, (top[1, p, h], acc[1, p, h])) for h in range(2)
        ]
        direct[1, p] = finish(1, p, results)
        forward[0, p] = pass_on(0, p, direct[0, p])
        if p == 0:
            for copy in w_parts:
                copy.wait_recv()
            w_shared = send(w_all.at[pl.ds(1, 3), rows], w_all.at[pl.ds(1, 3), rows], (partner, group))

    own_w.wait()
    for copy in [w_shared] + forward[0, 0] + forward[1, 0]:
        copy.wait_recv()
    total = project(1, (0, 0), (0, 1), (1, 0), (2, 0), (3, 0))
    other = project(0, (0, 0), (0, 1), (1, 0), (1, 1), (2, 0), (2, 1), (3, 0))
    for copy in forward[0, 1]:
        copy.wait_recv()
    mixed[inner] = (other + project(0, (3, 1))).astype(BF16)
    for copy in direct[1, 1]:
        copy.wait_recv()
    mixed[outer] = (total + project(1, (1, 1), (2, 1), (3, 1))).astype(BF16)
    for copy in sends:
        copy.wait_send()


def body(queries, keys, values, pairs, out_weight):
    own_frames, tokens, cols = queries.shape
    frames_axis = lax.axis_size("frame")
    groups = lax.axis_size("head")
    assert own_frames == 2 and cols == 4 * HD and groups == 4
    in_place = pl.BlockSpec(memory_space=pltpu.HBM)
    multiply_adds = 10 * 4 * tokens * tokens * (4 * HD + 4 * HD) + 2 * tokens * groups * cols * cols
    return pl.pallas_call(
        functools.partial(kernel, frames_axis, groups),
        out_shape=jax.ShapeDtypeStruct(queries.shape, BF16),
        in_specs=[in_place] * 3 + [pl.BlockSpec(memory_space=pltpu.VMEM), in_place],
        out_specs=pl.BlockSpec(memory_space=pltpu.VMEM),
        scratch_shapes=[
            pltpu.VMEM((2, tokens, cols), BF16),
            pltpu.VMEM((2, 2, 2, tokens, 2 * PAIR), BF16),
            pltpu.VMEM((6, 2, tokens, PAIR), BF16),
            pltpu.VMEM((6, 2, tokens, PAIR), BF16),
            pltpu.VMEM((2, 6, 8, PAIR), F32),
            pltpu.VMEM((2, 2, 2, tokens, 2 * PAIR), F32),
            pltpu.VMEM((2, 2, 2, tokens, PAIR), F32),
            pltpu.VMEM((4, 2, 2, tokens, PAIR), BF16),
            pltpu.VMEM((4, cols, cols), BF16),
            pltpu.SemaphoreType.DMA((35,)),
            pltpu.SemaphoreType.DMA((35,)),
            pltpu.SemaphoreType.DMA((10,)),
            pltpu.SemaphoreType.REGULAR,
        ],
        compiler_params=pltpu.CompilerParams(
            collective_id=0, has_side_effects=True, vmem_limit_bytes=62 * 2**20
        ),
        cost_estimate=pl.CostEstimate(
            flops=2 * multiply_adds, bytes_accessed=4 * queries.size * 2, transcendentals=0
        ),
    )(queries, keys, values, pairs.T, out_weight)


def solution(mesh):
    placed = (
        P("frame", None, "head"),
        P("frame", None, "head"),
        P("frame", None, "head"),
        P(),
        P("head", None),
    )
    return jax.shard_map(
        body, mesh=mesh, in_specs=placed, out_specs=P("frame", None, "head"), check_vma=False
    )
```

```python
import functools

import jax
import jax.numpy as jnp
from jax import lax
from jax.experimental import pallas as pl
from jax.experimental.pallas import tpu as pltpu
from jax.sharding import PartitionSpec as P

HD = 64
PAIR = 2 * HD
LOG2E = 1.4426950408889634
FAR = 1.0e5
GRANT = 107 * 2**19
RUN = 32
MESH = pl.DeviceIdType.MESH
F32 = jnp.float32
BF16 = jnp.bfloat16
ACROSS = (((1,), (1,)), ((), ()))

PARTNER_FAR, PARTNER_NEAR, INNER, OUTER, NEXT_NEAR, NEXT_FAR = range(6)


def kernel(
    frames_axis,
    groups,
    q_hbm,
    k_hbm,
    v_hbm,
    pairs_hbm,
    w_hbm,
    mixed,
    pairs_ref,
    q_raw,
    q_cut,
    k_all,
    v_all,
    penalty,
    acc,
    top,
    gathered,
    w_all,
    send_sem,
    recv_sem,
    local_sem,
    ready,
):
    tokens = q_hbm.shape[1]
    group_cols = q_hbm.shape[2]
    me = lax.axis_index("frame")
    group = lax.axis_index("head")
    core = lax.rem(me, 2)
    toward = 1 - 2 * core
    partner = me + toward
    beyond = lax.rem(me - toward + frames_axis, frames_axis)
    up = lax.rem(group + 1, groups)
    down = lax.rem(group + groups - 1, groups)
    across = lax.rem(group + 2, groups)
    outer = core
    inner = 1 - core
    late = lax.rem(me, RUN) == 0

    barrier = pltpu.get_barrier_semaphore()
    for device in ((partner, group), (me, up), (me, down), (me, across)):
        pl.semaphore_signal(barrier, inc=1, device_id=device, device_id_type=MESH)

    @pl.when(core == 0)
    def _():
        pl.semaphore_signal(barrier, inc=1, device_id=(beyond, group), device_id_type=MESH)

    def fetch(number, source, target):
        copy = pltpu.make_async_copy(source, target, local_sem.at[number])
        copy.start()
        return copy

    own_pairs = fetch(10, pairs_hbm, pairs_ref)
    own_q = fetch(0, q_hbm, q_raw)
    own_kv = []
    for slot, frame in ((INNER, inner), (OUTER, outer)):
        for p in range(2):
            for which, (source, target) in enumerate(((k_hbm, k_all), (v_hbm, v_all))):
                own_kv.append(
                    fetch(
                        1 + len(own_kv),
                        source.at[frame, :, pl.ds(p * PAIR, PAIR)],
                        target.at[slot, p],
                    )
                )
    own_w = fetch(
        9, w_hbm.at[:, pl.ds(pl.multiple_of(group * group_cols, group_cols), group_cols)], w_all.at[0]
    )

    pl.semaphore_wait(barrier, 4 + core)


    sends = []

    def prepare(source, target, device):
        number = len(sends)
        copy = pltpu.make_async_remote_copy(
            src_ref=source,
            dst_ref=target,
            send_sem=send_sem.at[number],
            recv_sem=recv_sem.at[number],
            device_id=device,
            device_id_type=MESH,
        )
        sends.append(copy)
        return copy

    def send(source, target, device):
        copy = prepare(source, target, device)
        copy.start()
        return copy

    next_kv = {}
    for p in range(2):
        for slot, frame in ((NEXT_NEAR, outer), (NEXT_FAR, inner)):
            next_kv[slot, p] = [
                prepare(
                    source.at[frame, :, pl.ds(p * PAIR, PAIR)],
                    target.at[slot, p],
                    (beyond, group),
                )
                for source, target in ((k_hbm, k_all), (v_hbm, v_all))
            ]

    @pl.when(core == 1)
    def _():
        pl.semaphore_signal(ready, inc=1, device_id=(beyond, group), device_id_type=MESH)
        for copies in next_kv.values():
            for copy in copies:
                copy.start()

    partner_kv = []
    for slot, frame in ((PARTNER_NEAR, inner), (PARTNER_FAR, outer)):
        for p in range(2):
            partner_kv += [
                send(
                    source.at[frame, :, pl.ds(p * PAIR, PAIR)],
                    target.at[slot, p],
                    (partner, group),
                )
                for source, target in ((k_hbm, k_all), (v_hbm, v_all))
            ]
    rows = pl.ds(pl.multiple_of(core * (group_cols // 2), group_cols // 2), group_cols // 2)
    w_parts = [
        send(
            w_hbm.at[rows, pl.ds(pl.multiple_of(there * group_cols, group_cols), group_cols)],
            w_all.at[place, rows],
            (me, there),
        )
        for place, there in ((1, up), (2, down), (3, across))
    ]

    own_pairs.wait()
    lower_end = pairs_ref[0:1, :]
    upper_end = pairs_ref[1:2, :]
    own_first = 2 * me

    def place_of(slot):
        steps = (3, 2, 1, 0, -1, -2)[slot]
        return own_first + outer + toward * steps

    for t, slot_q in enumerate((INNER, OUTER)):
        for slot in range(6):
            if slot == slot_q or abs(slot - slot_q) > 2:
                continue
            a, b = place_of(slot_q), place_of(slot)
            hit = (lower_end == jnp.minimum(a, b)) & (upper_end == jnp.maximum(a, b))
            missing = jnp.min(jnp.where(hit, 0.0, FAR).astype(F32), axis=1, keepdims=True)
            penalty[t, slot] = jnp.broadcast_to(missing, (8, PAIR))
        penalty[t, slot_q] = jnp.zeros((8, PAIR), F32)

    lane = lax.broadcasted_iota(jnp.int32, (tokens, PAIR), 1)
    first = lane < HD

    own_q.wait()
    for t, frame in enumerate((inner, outer)):
        for p in range(2):
            q = q_raw[frame, :, p * PAIR : (p + 1) * PAIR].astype(F32) * (0.125 * LOG2E)
            high = q.astype(BF16)
            low = (q - high.astype(F32)).astype(BF16)
            nothing = jnp.zeros_like(high)
            for h in range(2):
                mine = first if h == 0 else ~first
                q_cut[t, p, h, :, 0:PAIR] = jnp.where(mine, high, nothing)
                q_cut[t, p, h, :, PAIR : 2 * PAIR] = jnp.where(mine, low, nothing)

    def attend(t, p, h, low_slot, high_slot, old):
        count = high_slot - low_slot
        k = k_all[low_slot:high_slot, p].reshape(count * tokens, PAIR)
        v = v_all[low_slot:high_slot, p].reshape(count * tokens, PAIR)
        scores = lax.dot_general(
            q_cut[t, p, h], jnp.concatenate([k, k], 1), ACROSS, preferred_element_type=F32
        )
        highest = None
        for j in range(count):
            s = scores[:, j * tokens : (j + 1) * tokens]
            part = s[:, 0:PAIR]
            for c in range(1, tokens // PAIR):
                part = jnp.maximum(part, s[:, c * PAIR : (c + 1) * PAIR])
            part = part - penalty[t, low_slot + j, 0:1, :]
            highest = part if highest is None else jnp.maximum(highest, part)
        now = jnp.broadcast_to(jnp.max(highest, axis=1, keepdims=True), (tokens, PAIR))
        if old is not None:
            now = jnp.maximum(now, old[0])
        weights = []
        for j in range(count):
            less = now + penalty[t, low_slot + j, 0:1, :]
            for c in range(tokens // PAIR):
                at = j * tokens + c * PAIR
                weights.append(jnp.exp2((scores[:, at : at + PAIR] - less).astype(BF16)))
        summed = jnp.dot(
            jnp.concatenate(weights, 1),
            jnp.concatenate([v, jnp.ones_like(v)], 1),
            preferred_element_type=F32,
        )
        if old is not None:
            scale = jnp.exp2(old[0] - now)
            summed = summed + old[1] * jnp.concatenate([scale, scale], 1)
        return now, summed

    def start_beyond():
        pl.semaphore_wait(ready, 1)
        for copies in next_kv.values():
            for copy in copies:
                copy.start()

    @pl.when((core == 0) & ~late)
    def _():
        start_beyond()

    for copy in own_kv:
        copy.wait()

    def visit(p, reach, merge):
        for t, (low_slot, high_slot) in enumerate(reach):
            for h in range(2):
                old = (top[t, p, h], acc[t, p, h]) if merge else None
                now, summed = attend(t, p, h, low_slot, high_slot, old)
                top[t, p, h] = now
                acc[t, p, h] = summed

    def near_frames(p):
        visit(p, ((PARTNER_FAR, NEXT_NEAR), (PARTNER_NEAR, NEXT_NEAR)), False)

    direct, forward, only_late = {}, {}, []

    def finish(t, p, results):
        parts = [summed[:, 0:PAIR] / summed[:, PAIR : 2 * PAIR] for _, summed in results]
        gathered[0, t, p] = jnp.where(first, parts[0], parts[1]).astype(BF16)
        direct[t, p] = [
            send(gathered.at[0, t, p], gathered.at[place, t, p], (me, there))
            for place, there in ((1, up), (2, down))
        ]
        whole = prepare(gathered.at[0, t, p], gathered.at[3, t, p], (me, across))
        if (t, p) == (1, 1):
            whole.start()
        else:
            pl.when(late)(whole.start)
            only_late.append(whole)
        direct[t, p].append(whole)

    half = tokens // 2

    def pass_on(t, p):
        forward[t, p] = [
            prepare(
                gathered.at[1, t, p, pl.ds(0, half)],
                gathered.at[3, t, p, pl.ds(0, half)],
                (me, up),
            ),
            prepare(
                gathered.at[2, t, p, pl.ds(half, half)],
                gathered.at[3, t, p, pl.ds(half, half)],
                (me, down),
            ),
        ]

        @pl.when(~late)
        def _():
            for copy in direct[t, p][:2]:
                copy.wait_recv()
            for copy in forward[t, p]:
                copy.start()

    def settle(t, p):
        @pl.when(late)
        def _():
            for copy in direct[t, p]:
                copy.wait_recv()

        @pl.when(~late)
        def _():
            for copy in forward[t, p]:
                copy.wait_recv()

    def project(t, *parts):
        return jnp.dot(
            jnp.concatenate([gathered[source, t, p] for source, p in parts], 1),
            jnp.concatenate([w_all[source, p * PAIR : (p + 1) * PAIR, :] for source, p in parts], 0),
            preferred_element_type=F32,
        )

    for p in range(2):
        if p == 0:
            visit(0, ((INNER, NEXT_NEAR), (INNER, NEXT_NEAR)), False)
            for copy in partner_kv:
                copy.wait_recv()
            visit(0, ((PARTNER_FAR, INNER), (PARTNER_NEAR, INNER)), True)

            @pl.when(late)
            def _():
                near_frames(1)
                start_beyond()

        else:

            @pl.when(~late)
            def _():
                near_frames(1)

            pass_on(0, 0)
            pass_on(1, 0)
            for copy in w_parts:
                copy.wait_recv()
            w_shared = send(w_all.at[pl.ds(1, 3), rows], w_all.at[pl.ds(1, 3), rows], (partner, group))
        for copy in next_kv[NEXT_NEAR, p]:
            copy.wait_recv()
        results = [
            attend(0, p, h, NEXT_NEAR, NEXT_NEAR + 1, (top[0, p, h], acc[0, p, h])) for h in range(2)
        ]
        finish(0, p, results)
        for h in range(2):
            now, summed = attend(1, p, h, NEXT_NEAR, NEXT_NEAR + 1, (top[1, p, h], acc[1, p, h]))
            top[1, p, h] = now
            acc[1, p, h] = summed
        for copy in next_kv[NEXT_FAR, p]:
            copy.wait_recv()
        results = [
            attend(1, p, h, NEXT_FAR, NEXT_FAR + 1, (top[1, p, h], acc[1, p, h])) for h in range(2)
        ]
        finish(1, p, results)

    pass_on(0, 1)
    own_w.wait()
    w_shared.wait_recv()
    settle(0, 0)
    settle(1, 0)
    total = project(1, (0, 0), (0, 1), (1, 0), (2, 0), (3, 0))
    other = project(0, (0, 0), (0, 1), (1, 0), (2, 0), (3, 0))
    settle(0, 1)
    mixed[inner] = (other + project(0, (1, 1), (2, 1), (3, 1))).astype(BF16)
    for copy in direct[1, 1]:
        copy.wait_recv()
    mixed[outer] = (total + project(1, (1, 1), (2, 1), (3, 1))).astype(BF16)

    @pl.when(late)
    def _():
        for copy in only_late:
            copy.wait_send()

    @pl.when(~late)
    def _():
        for copies in forward.values():
            for copy in copies:
                copy.wait_send()

    not_all = only_late + [copy for copies in forward.values() for copy in copies]
    for copy in sends:
        if not any(copy is other_copy for other_copy in not_all):
            copy.wait_send()


def body(queries, keys, values, pairs, out_weight):
    own_frames, tokens, cols = queries.shape
    frames_axis = lax.axis_size("frame")
    groups = lax.axis_size("head")
    assert own_frames == 2 and cols == 4 * HD and groups == 4
    in_place = pl.BlockSpec(memory_space=pltpu.HBM)
    multiply_adds = 10 * 4 * tokens * tokens * (4 * HD + 4 * HD) + 2 * tokens * groups * cols * cols
    return pl.pallas_call(
        functools.partial(kernel, frames_axis, groups),
        out_shape=jax.ShapeDtypeStruct(queries.shape, BF16),
        in_specs=[in_place] * 5,
        out_specs=pl.BlockSpec(memory_space=pltpu.VMEM),
        scratch_shapes=[
            pltpu.VMEM(pairs.shape[::-1], jnp.int32),
            pltpu.VMEM((2, tokens, cols), BF16),
            pltpu.VMEM((2, 2, 2, tokens, 2 * PAIR), BF16),
            pltpu.VMEM((6, 2, tokens, PAIR), BF16),
            pltpu.VMEM((6, 2, tokens, PAIR), BF16),
            pltpu.VMEM((2, 6, 8, PAIR), F32),
            pltpu.VMEM((2, 2, 2, tokens, 2 * PAIR), F32),
            pltpu.VMEM((2, 2, 2, tokens, PAIR), F32),
            pltpu.VMEM((4, 2, 2, tokens, PAIR), BF16),
            pltpu.VMEM((4, cols, cols), BF16),
            pltpu.SemaphoreType.DMA((40,)),
            pltpu.SemaphoreType.DMA((40,)),
            pltpu.SemaphoreType.DMA((11,)),
            pltpu.SemaphoreType.REGULAR,
        ],
        compiler_params=pltpu.CompilerParams(
            collective_id=0, has_side_effects=True, vmem_limit_bytes=GRANT
        ),
        cost_estimate=pl.CostEstimate(
            flops=2 * multiply_adds, bytes_accessed=4 * queries.size * 2, transcendentals=0
        ),
    )(queries, keys, values, pairs.T, out_weight)


def solution(mesh):
    placed = (
        P("frame", None, "head"),
        P("frame", None, "head"),
        P("frame", None, "head"),
        P(),
        P("head", None),
    )
    return jax.shard_map(
        body, mesh=mesh, in_specs=placed, out_specs=P("frame", None, "head"), check_vma=False
    )
```

```python
import functools

import jax
import jax.numpy as jnp
from jax import lax
from jax.experimental import pallas as pl
from jax.experimental.pallas import tpu as pltpu
from jax.sharding import PartitionSpec as P

HD = 64
PAIR = 2 * HD
LOG2E = 1.4426950408889634
FAR = 1.0e5
GRANT = 107 * 2**19
RUN = 32
MESH = pl.DeviceIdType.MESH
F32 = jnp.float32
BF16 = jnp.bfloat16
ACROSS = (((1,), (1,)), ((), ()))

PARTNER_FAR, PARTNER_NEAR, INNER, OUTER, NEXT_NEAR, NEXT_FAR = range(6)


def kernel(
    frames_axis,
    groups,
    q_hbm,
    k_hbm,
    v_hbm,
    pairs_hbm,
    w_hbm,
    mixed,
    pairs_ref,
    q_raw,
    q_cut,
    k_all,
    v_all,
    penalty,
    acc,
    top,
    gathered,
    w_all,
    send_sem,
    recv_sem,
    local_sem,
    ready,
):
    tokens = q_hbm.shape[1]
    group_cols = q_hbm.shape[2]
    me = lax.axis_index("frame")
    group = lax.axis_index("head")
    core = lax.rem(me, 2)
    toward = 1 - 2 * core
    partner = me + toward
    beyond = lax.rem(me - toward + frames_axis, frames_axis)
    up = lax.rem(group + 1, groups)
    down = lax.rem(group + groups - 1, groups)
    across = lax.rem(group + 2, groups)
    outer = core
    inner = 1 - core
    first_of_all, last_of_all = me == 0, me == frames_axis - 1
    alone = first_of_all | last_of_all
    late = (lax.rem(me, RUN) == 0) & ~first_of_all

    barrier = pltpu.get_barrier_semaphore()
    for device in ((partner, group), (me, up), (me, down), (me, across)):
        pl.semaphore_signal(barrier, inc=1, device_id=device, device_id_type=MESH)

    @pl.when((core == 0) & ~first_of_all)
    def _():
        pl.semaphore_signal(barrier, inc=1, device_id=(beyond, group), device_id_type=MESH)

    def fetch(number, source, target):
        copy = pltpu.make_async_copy(source, target, local_sem.at[number])
        copy.start()
        return copy

    own_pairs = fetch(10, pairs_hbm, pairs_ref)
    own_q = fetch(0, q_hbm, q_raw)
    own_kv = []
    for slot, frame in ((INNER, inner), (OUTER, outer)):
        for p in range(2):
            for which, (source, target) in enumerate(((k_hbm, k_all), (v_hbm, v_all))):
                own_kv.append(
                    fetch(
                        1 + len(own_kv),
                        source.at[frame, :, pl.ds(p * PAIR, PAIR)],
                        target.at[slot, p],
                    )
                )
    own_w = fetch(
        9, w_hbm.at[:, pl.ds(pl.multiple_of(group * group_cols, group_cols), group_cols)], w_all.at[0]
    )

    @pl.when(alone)
    def _():
        for frames in (k_all, v_all):
            frames[NEXT_NEAR : NEXT_FAR + 1] = jnp.zeros((2,) + frames.shape[1:], BF16)

    pl.semaphore_wait(barrier, 4 + core - last_of_all.astype(jnp.int32))


    sends = []

    def prepare(source, target, device):
        number = len(sends)
        copy = pltpu.make_async_remote_copy(
            src_ref=source,
            dst_ref=target,
            send_sem=send_sem.at[number],
            recv_sem=recv_sem.at[number],
            device_id=device,
            device_id_type=MESH,
        )
        sends.append(copy)
        return copy

    def send(source, target, device):
        copy = prepare(source, target, device)
        copy.start()
        return copy

    next_kv = {}
    for p in range(2):
        for slot, frame in ((NEXT_NEAR, outer), (NEXT_FAR, inner)):
            next_kv[slot, p] = [
                prepare(
                    source.at[frame, :, pl.ds(p * PAIR, PAIR)],
                    target.at[slot, p],
                    (beyond, group),
                )
                for source, target in ((k_hbm, k_all), (v_hbm, v_all))
            ]

    @pl.when((core == 1) & ~last_of_all)
    def _():
        pl.semaphore_signal(ready, inc=1, device_id=(beyond, group), device_id_type=MESH)
        for copies in next_kv.values():
            for copy in copies:
                copy.start()

    partner_kv = []
    for slot, frame in ((PARTNER_NEAR, inner), (PARTNER_FAR, outer)):
        for p in range(2):
            partner_kv += [
                send(
                    source.at[frame, :, pl.ds(p * PAIR, PAIR)],
                    target.at[slot, p],
                    (partner, group),
                )
                for source, target in ((k_hbm, k_all), (v_hbm, v_all))
            ]
    rows = pl.ds(pl.multiple_of(core * (group_cols // 2), group_cols // 2), group_cols // 2)
    w_parts = [
        send(
            w_hbm.at[rows, pl.ds(pl.multiple_of(there * group_cols, group_cols), group_cols)],
            w_all.at[place, rows],
            (me, there),
        )
        for place, there in ((1, up), (2, down), (3, across))
    ]

    own_pairs.wait()
    lower_end = pairs_ref[0:1, :]
    upper_end = pairs_ref[1:2, :]
    own_first = 2 * me

    def place_of(slot):
        steps = (3, 2, 1, 0, -1, -2)[slot]
        return own_first + outer + toward * steps

    for t, slot_q in enumerate((INNER, OUTER)):
        for slot in range(6):
            if slot == slot_q or abs(slot - slot_q) > 2:
                continue
            a, b = place_of(slot_q), place_of(slot)
            hit = (lower_end == jnp.minimum(a, b)) & (upper_end == jnp.maximum(a, b))
            missing = jnp.min(jnp.where(hit, 0.0, FAR).astype(F32), axis=1, keepdims=True)
            penalty[t, slot] = jnp.broadcast_to(missing, (8, PAIR))
        penalty[t, slot_q] = jnp.zeros((8, PAIR), F32)

    lane = lax.broadcasted_iota(jnp.int32, (tokens, PAIR), 1)
    first = lane < HD

    own_q.wait()
    for t, frame in enumerate((inner, outer)):
        for p in range(2):
            q = q_raw[frame, :, p * PAIR : (p + 1) * PAIR].astype(F32) * (0.125 * LOG2E)
            high = q.astype(BF16)
            low = (q - high.astype(F32)).astype(BF16)
            nothing = jnp.zeros_like(high)
            for h in range(2):
                mine = first if h == 0 else ~first
                q_cut[t, p, h, :, 0:PAIR] = jnp.where(mine, high, nothing)
                q_cut[t, p, h, :, PAIR : 2 * PAIR] = jnp.where(mine, low, nothing)

    def weigh(t, p, h, low_slot, high_slot, old):
        count = high_slot - low_slot
        k = k_all[low_slot:high_slot, p].reshape(count * tokens, PAIR)
        scores = lax.dot_general(
            q_cut[t, p, h], jnp.concatenate([k, k], 1), ACROSS, preferred_element_type=F32
        )
        highest = None
        for j in range(count):
            s = scores[:, j * tokens : (j + 1) * tokens]
            part = s[:, 0:PAIR]
            for c in range(1, tokens // PAIR):
                part = jnp.maximum(part, s[:, c * PAIR : (c + 1) * PAIR])
            part = part - penalty[t, low_slot + j, 0:1, :]
            highest = part if highest is None else jnp.maximum(highest, part)
        now = jnp.broadcast_to(jnp.max(highest, axis=1, keepdims=True), (tokens, PAIR))
        if old is not None:
            now = jnp.maximum(now, old[0])
        weights = []
        for j in range(count):
            less = now + penalty[t, low_slot + j, 0:1, :]
            for c in range(tokens // PAIR):
                at = j * tokens + c * PAIR
                weights.append(jnp.exp2((scores[:, at : at + PAIR] - less).astype(BF16)))
        return now, jnp.concatenate(weights, 1)

    def add_up(p, low_slot, high_slot, old, now, weights):
        v = v_all[low_slot:high_slot, p].reshape((high_slot - low_slot) * tokens, PAIR)
        summed = jnp.dot(
            weights,
            jnp.concatenate([v, jnp.ones_like(v)], 1),
            preferred_element_type=F32,
        )
        if old is not None:
            scale = jnp.exp2(old[0] - now)
            summed = summed + old[1] * jnp.concatenate([scale, scale], 1)
        return now, summed

    def start_beyond():
        pl.semaphore_wait(ready, 1)
        for copies in next_kv.values():
            for copy in copies:
                copy.start()

    @pl.when((core == 0) & ~late & ~first_of_all)
    def _():
        start_beyond()

    for copy in own_kv:
        copy.wait()

    def attend(t, p, h, low_slot, high_slot, old):
        return add_up(p, low_slot, high_slot, old, *weigh(t, p, h, low_slot, high_slot, old))

    def attend_beyond(t, p, slot):
        olds = [(top[t, p, h], acc[t, p, h]) for h in range(2)]
        weighed = [weigh(t, p, h, slot, slot + 1, olds[h]) for h in range(2)]
        if t == slot - NEXT_NEAR:
            pl.when(~alone)(next_kv[slot, p][1].wait_recv)
        return [add_up(p, slot, slot + 1, old, *pair) for old, pair in zip(olds, weighed)]

    def visit(p, reach, merge):
        for t, (low_slot, high_slot) in enumerate(reach):
            for h in range(2):
                old = (top[t, p, h], acc[t, p, h]) if merge else None
                now, summed = attend(t, p, h, low_slot, high_slot, old)
                top[t, p, h] = now
                acc[t, p, h] = summed

    def near_frames(p):
        visit(p, ((PARTNER_FAR, NEXT_NEAR), (PARTNER_NEAR, NEXT_NEAR)), False)

    direct, forward, only_late = {}, {}, []

    def finish(t, p, results):
        parts = [summed[:, 0:PAIR] / summed[:, PAIR : 2 * PAIR] for _, summed in results]
        gathered[0, t, p] = jnp.where(first, parts[0], parts[1]).astype(BF16)
        direct[t, p] = [
            send(gathered.at[0, t, p], gathered.at[place, t, p], (me, there))
            for place, there in ((1, up), (2, down))
        ]
        whole = prepare(gathered.at[0, t, p], gathered.at[3, t, p], (me, across))
        if (t, p) == (1, 1):
            whole.start()
        else:
            pl.when(late)(whole.start)
            only_late.append(whole)
        direct[t, p].append(whole)

    half = tokens // 2

    def pass_on(t, p):
        forward[t, p] = [
            prepare(
                gathered.at[1, t, p, pl.ds(0, half)],
                gathered.at[3, t, p, pl.ds(0, half)],
                (me, up),
            ),
            prepare(
                gathered.at[2, t, p, pl.ds(half, half)],
                gathered.at[3, t, p, pl.ds(half, half)],
                (me, down),
            ),
        ]

        @pl.when(~late)
        def _():
            for copy in direct[t, p][:2]:
                copy.wait_recv()
            for copy in forward[t, p]:
                copy.start()

    def settle(t, p):
        @pl.when(late)
        def _():
            for copy in direct[t, p]:
                copy.wait_recv()

        @pl.when(~late)
        def _():
            for copy in forward[t, p]:
                copy.wait_recv()

    def project(t, *parts):
        return jnp.dot(
            jnp.concatenate([gathered[source, t, p] for source, p in parts], 1),
            jnp.concatenate([w_all[source, p * PAIR : (p + 1) * PAIR, :] for source, p in parts], 0),
            preferred_element_type=F32,
        )

    for p in range(2):
        if p == 0:
            visit(0, ((INNER, NEXT_NEAR), (INNER, NEXT_NEAR)), False)
            for copy in partner_kv:
                copy.wait_recv()
            visit(0, ((PARTNER_FAR, INNER), (PARTNER_NEAR, INNER)), True)

            @pl.when(late)
            def _():
                near_frames(1)
                start_beyond()

        else:

            @pl.when(~late)
            def _():
                near_frames(1)

            pass_on(0, 0)
            pass_on(1, 0)
            for copy in w_parts:
                copy.wait_recv()
            w_shared = send(w_all.at[pl.ds(1, 3), rows], w_all.at[pl.ds(1, 3), rows], (partner, group))
        pl.when(~alone)(next_kv[NEXT_NEAR, p][0].wait_recv)
        finish(0, p, attend_beyond(0, p, NEXT_NEAR))
        for h, (now, summed) in enumerate(attend_beyond(1, p, NEXT_NEAR)):
            top[1, p, h] = now
            acc[1, p, h] = summed
        pl.when(~alone)(next_kv[NEXT_FAR, p][0].wait_recv)
        finish(1, p, attend_beyond(1, p, NEXT_FAR))

    pass_on(0, 1)
    own_w.wait()
    w_shared.wait_recv()
    settle(0, 0)
    settle(1, 0)
    total = project(1, (0, 0), (0, 1), (1, 0), (2, 0), (3, 0))
    other = project(0, (0, 0), (0, 1), (1, 0), (2, 0), (3, 0))
    settle(0, 1)
    mixed[inner] = (other + project(0, (1, 1), (2, 1), (3, 1))).astype(BF16)
    for copy in direct[1, 1]:
        copy.wait_recv()
    mixed[outer] = (total + project(1, (1, 1), (2, 1), (3, 1))).astype(BF16)

    @pl.when(late)
    def _():
        for copy in only_late:
            copy.wait_send()

    @pl.when(~late)
    def _():
        for copies in forward.values():
            for copy in copies:
                copy.wait_send()

    @pl.when(~alone)
    def _():
        for copies in next_kv.values():
            for copy in copies:
                copy.wait_send()

    not_all = only_late + [copy for copies in next_kv.values() for copy in copies] + [copy for copies in forward.values() for copy in copies]
    for copy in sends:
        if not any(copy is other_copy for other_copy in not_all):
            copy.wait_send()


def body(queries, keys, values, pairs, out_weight):
    own_frames, tokens, cols = queries.shape
    frames_axis = lax.axis_size("frame")
    groups = lax.axis_size("head")
    assert own_frames == 2 and cols == 4 * HD and groups == 4
    in_place = pl.BlockSpec(memory_space=pltpu.HBM)
    multiply_adds = 10 * 4 * tokens * tokens * (4 * HD + 4 * HD) + 2 * tokens * groups * cols * cols
    return pl.pallas_call(
        functools.partial(kernel, frames_axis, groups),
        out_shape=jax.ShapeDtypeStruct(queries.shape, BF16),
        in_specs=[in_place] * 5,
        out_specs=pl.BlockSpec(memory_space=pltpu.VMEM),
        scratch_shapes=[
            pltpu.VMEM(pairs.shape[::-1], jnp.int32),
            pltpu.VMEM((2, tokens, cols), BF16),
            pltpu.VMEM((2, 2, 2, tokens, 2 * PAIR), BF16),
            pltpu.VMEM((6, 2, tokens, PAIR), BF16),
            pltpu.VMEM((6, 2, tokens, PAIR), BF16),
            pltpu.VMEM((2, 6, 8, PAIR), F32),
            pltpu.VMEM((2, 2, 2, tokens, 2 * PAIR), F32),
            pltpu.VMEM((2, 2, 2, tokens, PAIR), F32),
            pltpu.VMEM((4, 2, 2, tokens, PAIR), BF16),
            pltpu.VMEM((4, cols, cols), BF16),
            pltpu.SemaphoreType.DMA((40,)),
            pltpu.SemaphoreType.DMA((40,)),
            pltpu.SemaphoreType.DMA((11,)),
            pltpu.SemaphoreType.REGULAR,
        ],
        compiler_params=pltpu.CompilerParams(
            collective_id=0, has_side_effects=True, vmem_limit_bytes=GRANT
        ),
        cost_estimate=pl.CostEstimate(
            flops=2 * multiply_adds, bytes_accessed=4 * queries.size * 2, transcendentals=0
        ),
    )(queries, keys, values, pairs.T, out_weight)


def solution(mesh):
    placed = (
        P("frame", None, "head"),
        P("frame", None, "head"),
        P("frame", None, "head"),
        P(),
        P("head", None),
    )
    return jax.shard_map(
        body, mesh=mesh, in_specs=placed, out_specs=P("frame", None, "head"), check_vma=False
    )
```

```python
import functools

import jax
import jax.numpy as jnp
from jax import lax
from jax.experimental import pallas as pl
from jax.experimental.pallas import tpu as pltpu
from jax.sharding import PartitionSpec as P

HD = 64
PAIR = 2 * HD
LOG2E = 1.4426950408889634
FAR = 1.0e5
GRANT = 107 * 2**19
RUN = 32
MESH = pl.DeviceIdType.MESH
F32 = jnp.float32
BF16 = jnp.bfloat16
ACROSS = (((1,), (1,)), ((), ()))

PARTNER_FAR, PARTNER_NEAR, INNER, OUTER, NEXT_NEAR, NEXT_FAR = range(6)


def kernel(
    frames_axis,
    groups,
    q_hbm,
    k_hbm,
    v_hbm,
    pairs_hbm,
    w_hbm,
    mixed,
    pairs_ref,
    q_raw,
    q_cut,
    k_all,
    v_all,
    penalty,
    acc,
    top,
    gathered,
    w_all,
    send_sem,
    recv_sem,
    local_sem,
    ready,
):
    tokens = q_hbm.shape[1]
    group_cols = q_hbm.shape[2]
    me = lax.axis_index("frame")
    group = lax.axis_index("head")
    core = lax.rem(me, 2)
    toward = 1 - 2 * core
    partner = me + toward
    beyond = lax.rem(me - toward + frames_axis, frames_axis)
    up = lax.rem(group + 1, groups)
    down = lax.rem(group + groups - 1, groups)
    across = lax.rem(group + 2, groups)
    outer = core
    inner = 1 - core
    first_of_all, last_of_all = me == 0, me == frames_axis - 1
    alone = first_of_all | last_of_all
    late = (lax.rem(me, RUN) == 0) & ~first_of_all

    barrier = pltpu.get_barrier_semaphore()
    for device in ((partner, group), (me, up), (me, down), (me, across)):
        pl.semaphore_signal(barrier, inc=1, device_id=device, device_id_type=MESH)

    @pl.when((core == 0) & ~first_of_all)
    def _():
        pl.semaphore_signal(barrier, inc=1, device_id=(beyond, group), device_id_type=MESH)

    def fetch(number, source, target):
        copy = pltpu.make_async_copy(source, target, local_sem.at[number])
        copy.start()
        return copy

    own_pairs = fetch(10, pairs_hbm, pairs_ref)
    own_q = fetch(0, q_hbm, q_raw)
    own_kv = []
    for slot, frame in ((INNER, inner), (OUTER, outer)):
        for p in range(2):
            for which, (source, target) in enumerate(((k_hbm, k_all), (v_hbm, v_all))):
                own_kv.append(
                    fetch(
                        1 + len(own_kv),
                        source.at[frame, :, pl.ds(p * PAIR, PAIR)],
                        target.at[slot, p],
                    )
                )
    own_w = fetch(
        9, w_hbm.at[:, pl.ds(pl.multiple_of(group * group_cols, group_cols), group_cols)], w_all.at[0]
    )

    @pl.when(alone)
    def _():
        for frames in (k_all, v_all):
            frames[NEXT_NEAR : NEXT_FAR + 1] = jnp.zeros((2,) + frames.shape[1:], BF16)

    pl.semaphore_wait(barrier, 4 + core - last_of_all.astype(jnp.int32))


    sends = []

    def prepare(source, target, device):
        number = len(sends)
        copy = pltpu.make_async_remote_copy(
            src_ref=source,
            dst_ref=target,
            send_sem=send_sem.at[number],
            recv_sem=recv_sem.at[number],
            device_id=device,
            device_id_type=MESH,
        )
        sends.append(copy)
        return copy

    def send(source, target, device):
        copy = prepare(source, target, device)
        copy.start()
        return copy

    next_kv = {}
    for p in range(2):
        for slot, frame in ((NEXT_NEAR, outer), (NEXT_FAR, inner)):
            next_kv[slot, p] = [
                prepare(
                    source.at[frame, :, pl.ds(p * PAIR, PAIR)],
                    target.at[slot, p],
                    (beyond, group),
                )
                for source, target in ((k_hbm, k_all), (v_hbm, v_all))
            ]

    @pl.when((core == 1) & ~last_of_all)
    def _():
        pl.semaphore_signal(ready, inc=1, device_id=(beyond, group), device_id_type=MESH)
        for copies in next_kv.values():
            for copy in copies:
                copy.start()

    partner_kv = []
    for slot, frame in ((PARTNER_NEAR, inner), (PARTNER_FAR, outer)):
        for p in range(2):
            partner_kv += [
                send(
                    source.at[frame, :, pl.ds(p * PAIR, PAIR)],
                    target.at[slot, p],
                    (partner, group),
                )
                for source, target in ((k_hbm, k_all), (v_hbm, v_all))
            ]
    rows = pl.ds(pl.multiple_of(core * (group_cols // 2), group_cols // 2), group_cols // 2)
    w_parts = [
        send(
            w_hbm.at[rows, pl.ds(pl.multiple_of(there * group_cols, group_cols), group_cols)],
            w_all.at[place, rows],
            (me, there),
        )
        for place, there in ((1, up), (2, down), (3, across))
    ]

    own_pairs.wait()
    lower_end = pairs_ref[0:1, :]
    upper_end = pairs_ref[1:2, :]
    own_first = 2 * me

    def place_of(slot):
        steps = (3, 2, 1, 0, -1, -2)[slot]
        return own_first + outer + toward * steps

    for t, slot_q in enumerate((INNER, OUTER)):
        for slot in range(6):
            if slot == slot_q or abs(slot - slot_q) > 2:
                continue
            a, b = place_of(slot_q), place_of(slot)
            hit = (lower_end == jnp.minimum(a, b)) & (upper_end == jnp.maximum(a, b))
            missing = jnp.min(jnp.where(hit, 0.0, FAR).astype(F32), axis=1, keepdims=True)
            penalty[t, slot] = jnp.broadcast_to(missing, (8, PAIR))
        penalty[t, slot_q] = jnp.zeros((8, PAIR), F32)

    lane = lax.broadcasted_iota(jnp.int32, (tokens, PAIR), 1)
    first = lane < HD

    own_q.wait()
    for t, frame in enumerate((inner, outer)):
        for p in range(2):
            q = q_raw[frame, :, p * PAIR : (p + 1) * PAIR].astype(F32) * (0.125 * LOG2E)
            high = q.astype(BF16)
            low = (q - high.astype(F32)).astype(BF16)
            nothing = jnp.zeros_like(high)
            for h in range(2):
                mine = first if h == 0 else ~first
                q_cut[t, p, h, :, 0:PAIR] = jnp.where(mine, high, nothing)
                q_cut[t, p, h, :, PAIR : 2 * PAIR] = jnp.where(mine, low, nothing)

    def weigh(t, p, h, low_slot, high_slot, old):
        count = high_slot - low_slot
        k = k_all[low_slot:high_slot, p].reshape(count * tokens, PAIR)
        scores = lax.dot_general(
            q_cut[t, p, h], jnp.concatenate([k, k], 1), ACROSS, preferred_element_type=F32
        )
        highest = None
        for j in range(count):
            s = scores[:, j * tokens : (j + 1) * tokens]
            part = s[:, 0:PAIR]
            for c in range(1, tokens // PAIR):
                part = jnp.maximum(part, s[:, c * PAIR : (c + 1) * PAIR])
            part = part - penalty[t, low_slot + j, 0:1, :]
            highest = part if highest is None else jnp.maximum(highest, part)
        now = jnp.broadcast_to(jnp.max(highest, axis=1, keepdims=True), (tokens, PAIR))
        if old is not None:
            now = jnp.maximum(now, old[0])
        weights = []
        for j in range(count):
            less = now + penalty[t, low_slot + j, 0:1, :]
            for c in range(tokens // PAIR):
                at = j * tokens + c * PAIR
                weights.append(jnp.exp2((scores[:, at : at + PAIR] - less).astype(BF16)))
        return now, jnp.concatenate(weights, 1)

    def add_up(p, low_slot, high_slot, old, now, weights):
        v = v_all[low_slot:high_slot, p].reshape((high_slot - low_slot) * tokens, PAIR)
        summed = jnp.dot(
            weights,
            jnp.concatenate([v, jnp.ones_like(v)], 1),
            preferred_element_type=F32,
        )
        if old is not None:
            scale = jnp.exp2(old[0] - now)
            summed = summed + old[1] * jnp.concatenate([scale, scale], 1)
        return now, summed

    def start_beyond():
        pl.semaphore_wait(ready, 1)
        for copies in next_kv.values():
            for copy in copies:
                copy.start()

    @pl.when((core == 0) & ~late & ~first_of_all)
    def _():
        start_beyond()

    for copy in own_kv:
        copy.wait()

    def attend(t, p, h, low_slot, high_slot, old):
        return add_up(p, low_slot, high_slot, old, *weigh(t, p, h, low_slot, high_slot, old))

    def attend_beyond(t, p, slot):
        olds = [(top[t, p, h], acc[t, p, h]) for h in range(2)]
        weighed = [weigh(t, p, h, slot, slot + 1, olds[h]) for h in range(2)]
        if t == slot - NEXT_NEAR:
            pl.when(~alone)(next_kv[slot, p][1].wait_recv)
        return [add_up(p, slot, slot + 1, old, *pair) for old, pair in zip(olds, weighed)]

    def visit(p, reach, merge):
        for t, (low_slot, high_slot) in enumerate(reach):
            for h in range(2):
                old = (top[t, p, h], acc[t, p, h]) if merge else None
                now, summed = attend(t, p, h, low_slot, high_slot, old)
                top[t, p, h] = now
                acc[t, p, h] = summed

    def near_frames(p):
        visit(p, ((PARTNER_FAR, NEXT_NEAR), (PARTNER_NEAR, NEXT_NEAR)), False)

    direct, forward, only_late = {}, {}, []

    def finish(t, p, results):
        parts = [summed[:, 0:PAIR] / summed[:, PAIR : 2 * PAIR] for _, summed in results]
        gathered[0, t, p] = jnp.where(first, parts[0], parts[1]).astype(BF16)
        whole = prepare(gathered.at[0, t, p], gathered.at[3, t, p], (me, across))
        if (t, p) == (1, 1):
            whole.start()
        else:
            pl.when(late)(whole.start)
            only_late.append(whole)
        direct[t, p] = [
            send(gathered.at[0, t, p], gathered.at[place, t, p], (me, there))
            for place, there in ((1, up), (2, down))
        ] + [whole]

    half = tokens // 2

    def pass_on(t, p):
        forward[t, p] = [
            prepare(
                gathered.at[1, t, p, pl.ds(0, half)],
                gathered.at[3, t, p, pl.ds(0, half)],
                (me, up),
            ),
            prepare(
                gathered.at[2, t, p, pl.ds(half, half)],
                gathered.at[3, t, p, pl.ds(half, half)],
                (me, down),
            ),
        ]

        @pl.when(~late)
        def _():
            for copy in direct[t, p][:2]:
                copy.wait_recv()
            for copy in forward[t, p]:
                copy.start()

    def settle(t, p):
        @pl.when(late)
        def _():
            for copy in direct[t, p]:
                copy.wait_recv()

        @pl.when(~late)
        def _():
            for copy in forward[t, p]:
                copy.wait_recv()

    def project(t, *parts):
        return jnp.dot(
            jnp.concatenate([gathered[source, t, p] for source, p in parts], 1),
            jnp.concatenate([w_all[source, p * PAIR : (p + 1) * PAIR, :] for source, p in parts], 0),
            preferred_element_type=F32,
        )

    for p in range(2):
        if p == 0:
            visit(0, ((INNER, NEXT_NEAR), (INNER, NEXT_NEAR)), False)
            for copy in partner_kv:
                copy.wait_recv()
            visit(0, ((PARTNER_FAR, INNER), (PARTNER_NEAR, INNER)), True)

            @pl.when(late)
            def _():
                near_frames(1)
                start_beyond()

        else:

            @pl.when(~late)
            def _():
                near_frames(1)

            pass_on(0, 0)
            pass_on(1, 0)
            for copy in w_parts:
                copy.wait_recv()
            w_shared = send(w_all.at[pl.ds(1, 3), rows], w_all.at[pl.ds(1, 3), rows], (partner, group))
        pl.when(~alone)(next_kv[NEXT_NEAR, p][0].wait_recv)
        finish(0, p, attend_beyond(0, p, NEXT_NEAR))
        for h, (now, summed) in enumerate(attend_beyond(1, p, NEXT_NEAR)):
            top[1, p, h] = now
            acc[1, p, h] = summed
        pl.when(~alone)(next_kv[NEXT_FAR, p][0].wait_recv)
        finish(1, p, attend_beyond(1, p, NEXT_FAR))

    pass_on(0, 1)
    own_w.wait()
    w_shared.wait_recv()
    settle(0, 0)
    settle(1, 0)
    total = project(1, (0, 0), (0, 1), (1, 0), (2, 0), (3, 0))
    other = project(0, (0, 0), (0, 1), (1, 0), (2, 0), (3, 0))
    settle(0, 1)
    mixed[inner] = (other + project(0, (1, 1), (2, 1), (3, 1))).astype(BF16)
    for copy in direct[1, 1]:
        copy.wait_recv()
    mixed[outer] = (total + project(1, (1, 1), (2, 1), (3, 1))).astype(BF16)

    @pl.when(late)
    def _():
        for copy in only_late:
            copy.wait_send()

    @pl.when(~late)
    def _():
        for copies in forward.values():
            for copy in copies:
                copy.wait_send()

    @pl.when(~alone)
    def _():
        for copies in next_kv.values():
            for copy in copies:
                copy.wait_send()

    not_all = only_late + [copy for copies in next_kv.values() for copy in copies] + [copy for copies in forward.values() for copy in copies]
    for copy in sends:
        if not any(copy is other_copy for other_copy in not_all):
            copy.wait_send()


def body(queries, keys, values, pairs, out_weight):
    own_frames, tokens, cols = queries.shape
    frames_axis = lax.axis_size("frame")
    groups = lax.axis_size("head")
    assert own_frames == 2 and cols == 4 * HD and groups == 4
    in_place = pl.BlockSpec(memory_space=pltpu.HBM)
    multiply_adds = 10 * 4 * tokens * tokens * (4 * HD + 4 * HD) + 2 * tokens * groups * cols * cols
    return pl.pallas_call(
        functools.partial(kernel, frames_axis, groups),
        out_shape=jax.ShapeDtypeStruct(queries.shape, BF16),
        in_specs=[in_place] * 5,
        out_specs=pl.BlockSpec(memory_space=pltpu.VMEM),
        scratch_shapes=[
            pltpu.VMEM(pairs.shape[::-1], jnp.int32),
            pltpu.VMEM((2, tokens, cols), BF16),
            pltpu.VMEM((2, 2, 2, tokens, 2 * PAIR), BF16),
            pltpu.VMEM((6, 2, tokens, PAIR), BF16),
            pltpu.VMEM((6, 2, tokens, PAIR), BF16),
            pltpu.VMEM((2, 6, 8, PAIR), F32),
            pltpu.VMEM((2, 2, 2, tokens, 2 * PAIR), F32),
            pltpu.VMEM((2, 2, 2, tokens, PAIR), F32),
            pltpu.VMEM((4, 2, 2, tokens, PAIR), BF16),
            pltpu.VMEM((4, cols, cols), BF16),
            pltpu.SemaphoreType.DMA((40,)),
            pltpu.SemaphoreType.DMA((40,)),
            pltpu.SemaphoreType.DMA((11,)),
            pltpu.SemaphoreType.REGULAR,
        ],
        compiler_params=pltpu.CompilerParams(
            collective_id=0, has_side_effects=True, vmem_limit_bytes=GRANT
        ),
        cost_estimate=pl.CostEstimate(
            flops=2 * multiply_adds, bytes_accessed=4 * queries.size * 2, transcendentals=0
        ),
    )(queries, keys, values, pairs.T, out_weight)


def solution(mesh):
    placed = (
        P("frame", None, "head"),
        P("frame", None, "head"),
        P("frame", None, "head"),
        P(),
        P("head", None),
    )
    return jax.shard_map(
        body, mesh=mesh, in_specs=placed, out_specs=P("frame", None, "head"), check_vma=False
    )
```
